32 devices in a mesh: groups: 2 (over y), tensor: 8 (over z, x), store: 2 (over core).
Axes of the slice: x: 2, y: 2, z: 4, core: 2. Of those that a mesh axis runs over, the one named last changes fastest.
Arguments:
- inputs: bfloat16 [4, 1024, 8192], P('groups', 'store', 'tensor'), parts along dimension 0, may hold values from -6 to 6
- base_up_matrix: bfloat16 [8192, 28672], P(None, 'tensor'), may hold values from -0.0625 to 0.0625
- adapter_shrink_weight: bfloat16 [64, 64, 8192], P('store', None, 'tensor'), may hold values from -0.0625 to 0.0625
- adapter_expand_weight: bfloat16 [64, 64, 28672], P('store', None, 'tensor'), may hold values from -0.75 to 0.75
- block_adapter_index: int32 [4, 8], P('groups'), parts along dimension 0, may hold values from 0 to 63
Outputs:
- projected: bfloat16 [4, 1024, 28672], P('groups', 'store', 'tensor'), parts along dimension 0
The draws below stay inside these ranges and needn't reach their ends.
There are 2 independent parts, one for each index of `groups`. The reference program is written for one: setup_inputs(seed, part) draws one part's arguments, and reference() takes and returns one part's arrays. A program takes and returns all parts, laid end to end along the dimension named above; an argument that names none is the same for every part. Nothing has to cross between parts.
All inputs are finite; a program needn't handle non-finite values.
Results may differ from the reference program's by a relative error of at most 0.0038.
Values may be sent and summed in bfloat16 or wider, within the bound.
A program may use at most 256 MiB of HBM per device.

```python
import math
import jax
import jax.numpy as jnp
import numpy as np

MODEL_WIDTH = 8192
HIDDEN_UNITS = 28672
ADAPTER_RANK = 64
STEPS = 2
ADAPTER_COUNT = 64
BLOCKS = 8
STEP_ROWS = 1024


def set_ends(values, stream_key, smallest, high):
    longest = values.shape.index(max(values.shape))
    spots = []
    for shift in (0, 1):
        where = [jax.random.randint(jax.random.fold_in(stream_key, axis), (), 0, length) for axis, length in enumerate(values.shape)]
        where[longest] = (where[longest] + shift) % values.shape[longest]
        spots.append(tuple(where))
    return values.at[spots[0]].set(smallest).at[spots[1]].set(high)


def block_scale(key, shape, shards, smallest, high):
    def one(axis_at, blocks):
        heights = jax.random.uniform(jax.random.fold_in(jax.random.fold_in(key, 6), axis_at), (blocks,), jnp.float32, smallest / len(shards), high / len(shards))
        return jnp.repeat(jnp.exp(heights), shape[axis_at] // blocks).reshape((-1,) + (1,) * (len(shape) - axis_at - 1))

    level = one(*shards[0])
    for cut in shards[1:]:
        level = level * one(*cut)
    return level


def rank_bounds(number_of, skew):
    weights = [(1 << 20) // math.isqrt(grade ** skew) + 1 for grade in range(1, number_of + 1)]
    deviation = 1 + sum(weights) // (1 << 30)
    return np.cumsum(np.array([max(1, weight // deviation) for weight in weights]))


def ranked(own_key, extent, count, skew):
    grid = rank_bounds(count, skew)
    pick = jax.random.randint(jax.random.fold_in(own_key, 1), extent, 0, int(grid[count - 1]))
    standing = jnp.searchsorted(jnp.asarray(grid, jnp.int32), pick, side="right")
    return jax.random.permutation(jax.random.fold_in(own_key, 2), count)[standing].astype(jnp.int32)


def centred(stream_key, dims, scale, limit, split=(), dtype=jnp.bfloat16):
    loudness = block_scale(stream_key, dims, split, -0.22, 0.18) if split else 1.0
    result = jax.random.normal(stream_key, dims, jnp.float32) * scale * loudness
    return jnp.minimum(jnp.maximum(result, -limit), limit).astype(dtype)


def setup_inputs(seed: int = 0, part: int = 0) -> dict:
    seeds = jax.random.split(jax.random.key(seed), 6)
    own_keys = jax.random.split(jax.random.fold_in(seeds[5], part), 6)
    return {
        "inputs": centred(own_keys[0], (STEPS, STEP_ROWS, MODEL_WIDTH), 1.0, 6.0, ((1, 2), (2, 8))),
        "base_up_matrix": centred(seeds[1], (MODEL_WIDTH, HIDDEN_UNITS), MODEL_WIDTH ** -0.5, 0.0625, ((1, 8),)),
        "adapter_shrink_weight": centred(seeds[2], (ADAPTER_COUNT, ADAPTER_RANK, MODEL_WIDTH), MODEL_WIDTH ** -0.5, 0.0625, ((0, 2), (2, 8))),
        "adapter_expand_weight": centred(seeds[3], (ADAPTER_COUNT, ADAPTER_RANK, HIDDEN_UNITS), ADAPTER_RANK ** -0.5, 0.75, ((0, 2), (2, 8))),
        "block_adapter_index": set_ends(ranked(own_keys[4], (STEPS, BLOCKS), ADAPTER_COUNT, 2), jax.random.fold_in(own_keys[4], 3), 0, ADAPTER_COUNT - 1).astype(jnp.int32),
    }


def reference(inputs, base_up_matrix, adapter_shrink_weight, adapter_expand_weight, block_adapter_index):
    step_count, row_count, model_width = inputs.shape
    block_count = block_adapter_index.shape[1]
    block_rows = row_count // block_count
    base_out = jnp.dot(inputs.reshape(step_count * row_count, model_width), base_up_matrix, preferred_element_type=jnp.float32)
    base_out = base_out.reshape(step_count, row_count, -1)
    row_blocks = inputs.reshape(step_count, block_count, block_rows, model_width).astype(jnp.float32)
    shrink_matrices = jnp.take(adapter_shrink_weight, block_adapter_index, axis=0).astype(jnp.float32)
    low_rank = jnp.einsum('sbtd,sbrd->sbrt', row_blocks, shrink_matrices).astype(jnp.bfloat16)
    expand_matrices = jnp.take(adapter_expand_weight, block_adapter_index, axis=0).astype(jnp.float32)
    adapter_out = jnp.einsum('sbrt,sbrf->sbtf', low_rank.astype(jnp.float32), expand_matrices)
    adapter_out = adapter_out.reshape(step_count, row_count, -1)
    return (base_out + adapter_out).astype(jnp.bfloat16)
```

```python
import functools

import jax
import jax.numpy as jnp
from jax import lax
from jax.experimental import pallas as pl
from jax.experimental.pallas import tpu as pltpu
from jax.sharding import PartitionSpec as P

MESH = pl.DeviceIdType.MESH
F32 = jnp.float32
BF16 = jnp.bfloat16
PIECES = 8
TILE = 256


def kernel(
    x_ref, base_ref, down_mine, down_send, up_mine, up_send,
    out_ref,
    xbuf, total, wbuf, down, up, part, gathered, ranks,
    send_sem, recv_sem, w_sem, local_sem, pair_send, pair_recv,
    rs_send, rs_recv, ag_send, ag_recv, out_sem,
):
    n = lax.axis_size("tensor")
    t = lax.axis_index("tensor")
    core = lax.axis_index("store")
    z, x = t // 2, t % 2
    sign = jnp.where(z < 2, 1, -1)
    is_end = (z == 0) | (z == 3)
    far, near, across = t + 2 * sign, t - 2 * sign, z * 2 + 1 - x
    rank = down.shape[1] // 2
    depth = xbuf.shape[2]
    tiles = total.shape[1] // TILE

    barrier = pltpu.get_barrier_semaphore()
    for d in range(1, n):
        pl.semaphore_signal(
            barrier, inc=1, device_id={"tensor": lax.rem(t + d, n)}, device_id_type=MESH
        )
    pl.semaphore_signal(barrier, inc=1, device_id={"store": 1 - core}, device_id_type=MESH)

    own_x = pltpu.make_async_copy(x_ref, xbuf.at[pl.ds(t * PIECES, PIECES)], local_sem.at[0])
    own_x.start()

    def load_w(share, slot):
        return pltpu.make_async_copy(
            base_ref.at[pl.ds(pl.multiple_of(share * depth, depth), depth)],
            wbuf.at[slot],
            w_sem.at[slot],
        )

    def share(dz, other):
        return (z + dz) * 2 + (1 - x if other else x)

    own_down = pltpu.make_async_copy(down_mine, down.at[:, pl.ds(0, rank)], local_sem.at[1])
    own_up = pltpu.make_async_copy(up_mine, up.at[:, pl.ds(0, rank)], local_sem.at[2])
    pair_down = pltpu.make_async_remote_copy(
        src_ref=down_send, dst_ref=down.at[:, pl.ds(rank, rank)],
        send_sem=pair_send.at[0], recv_sem=pair_recv.at[0],
        device_id={"store": 1 - core}, device_id_type=MESH,
    )
    pair_up = pltpu.make_async_remote_copy(
        src_ref=up_send, dst_ref=up.at[:, pl.ds(rank, rank)],
        send_sem=pair_send.at[1], recv_sem=pair_recv.at[1],
        device_id={"store": 1 - core}, device_id_type=MESH,
    )

    def piece(which, p, way, target):
        i = which * PIECES + p
        return pltpu.make_async_remote_copy(
            src_ref=xbuf.at[i], dst_ref=xbuf.at[i],
            send_sem=send_sem.at[way], recv_sem=recv_sem.at[i],
            device_id={"tensor": target}, device_id_type=MESH,
        )

    def to_far(which, p):
        piece(which, p, 0, far).start()

    def to_near(which, p):
        piece(which, p, 1, near).start()

    def to_across(which, p):
        piece(which, p, 2, across).start()

    def got(which, p):
        piece(which, p, 2, across).wait_recv()

    def drain(way, count):
        view = xbuf.at[pl.ds(0, count)]
        pltpu.make_async_remote_copy(
            src_ref=view, dst_ref=view, send_sem=send_sem.at[way], recv_sem=recv_sem.at[0],
            device_id={"tensor": across}, device_id_type=MESH,
        ).wait_send()

    def product(which, first, count, slot, tile):
        lhs = xbuf[pl.ds(which * PIECES + first, count)].reshape(count * xbuf.shape[1], depth)
        columns = pl.ds(pl.multiple_of(tile * TILE, TILE), TILE)
        return jnp.dot(lhs, wbuf[slot, :, columns], preferred_element_type=F32)

    def add(which, first, count, slot, tile):
        rows = pl.ds(pl.multiple_of(first * xbuf.shape[1], xbuf.shape[1]), count * xbuf.shape[1])
        columns = pl.ds(pl.multiple_of(tile * TILE, TILE), TILE)
        total[rows, columns] += product(which, first, count, slot, tile)

    def set_own(tile):
        columns = pl.ds(pl.multiple_of(tile * TILE, TILE), TILE)
        total[:, columns] = product(t, 0, PIECES, 0, tile)

    def own_tiles(p):
        @pl.when(p == 0)
        def _():
            load_w(t, 0).wait()

        @pl.when(p < tiles // 2)
        def _():
            set_own(2 * p)
            set_own(2 * p + 1)

    def run(low, high, order):
        def one(u, carry):
            which, slot = order[0]
            for k in range(1, len(order)):
                which = jnp.where(u >= k * tiles, order[k][0], which)
                slot = jnp.where(u >= k * tiles, order[k][1], slot)

            @pl.when(u % tiles == 0)
            def _():
                load_w(which, slot).wait()

            add(which, 0, PIECES, slot, u % tiles)
            return carry

        top = len(order) * tiles
        lax.fori_loop(jnp.minimum(low, top), jnp.minimum(high, top), one, 0)

    def out_copy(h):
        rows = pl.ds(pl.multiple_of(h * 256, 256), 256)
        return pltpu.make_async_copy(wbuf.at[2, rows], out_ref.at[rows], out_sem.at[h])

    def finish(which, slot, h):
        def one(tile, carry):
            rows = pl.ds(pl.multiple_of(h * 256, 256), 256)
            columns = pl.ds(pl.multiple_of(tile * TILE, TILE), TILE)
            value = total[rows, columns] + product(which, 2 * h, 2, slot, tile)
            wbuf[2, rows, columns] = value.astype(BF16)
            return carry

        lax.fori_loop(0, tiles, one, 0)
        out_copy(h).start()

    def rank_partial():
        own_down.wait()
        pair_down.wait_recv()

        def one(b, carry):
            both = lax.dot_general(
                down[b], xbuf[t * PIECES + b], (((1,), (1,)), ((), ())), preferred_element_type=F32
            )
            part[b] = both[:rank] + both[rank:]
            return carry

        lax.fori_loop(0, n, one, 0)

        def send(d, carry):
            rs_copy(d).start()
            return carry

        lax.fori_loop(1, n, send, 0)

    def rs_copy(d):
        target = lax.rem(t + d, n)
        return pltpu.make_async_remote_copy(
            src_ref=part.at[target], dst_ref=gathered.at[t],
            send_sem=rs_send.at[d], recv_sem=rs_recv.at[d],
            device_id={"tensor": target}, device_id_type=MESH,
        )

    def ag_copy(d):
        target = lax.rem(t + d, n)
        return pltpu.make_async_remote_copy(
            src_ref=ranks.at[t], dst_ref=ranks.at[t],
            send_sem=ag_send.at[d], recv_sem=ag_recv.at[d],
            device_id={"tensor": target}, device_id_type=MESH,
        )

    def rank_sum():
        def got_part(d, value):
            rs_copy(d).wait_recv()
            return value + gathered[lax.rem(t - d + n, n)]

        value = lax.fori_loop(1, n, got_part, part[t])
        ranks[t] = value.astype(BF16)

        def send(d, carry):
            ag_copy(d).start()
            return carry

        lax.fori_loop(1, n, send, 0)

    def expand():
        own_up.wait()
        pair_up.wait_recv()

        def got_rank(d, carry):
            ag_copy(d).wait_recv()
            return carry

        lax.fori_loop(1, n, got_rank, 0)

        def one(b, carry):
            low = ranks[b].astype(F32).T.astype(BF16)
            both = jnp.concatenate([low, low], axis=1)
            rows = pl.ds(pl.multiple_of(b * 128, 128), 128)

            def tile(k, inner):
                columns = pl.ds(pl.multiple_of(k * TILE, TILE), TILE)
                total[rows, columns] += jnp.dot(
                    both, up[b, :, columns], preferred_element_type=F32
                )
                return inner

            lax.fori_loop(0, tiles, tile, 0)
            return carry

        lax.fori_loop(0, n, one, 0)

    def loop(count, body):
        def step(p, carry):
            body(p)
            return carry

        lax.fori_loop(0, count, step, 0)

    load_w(t, 0).start()
    own_down.start()
    own_up.start()
    pl.semaphore_wait(barrier, n)
    own_x.wait()

    @pl.when(is_end)
    def _():
        def first(p):
            to_far(t, p)
            to_across(t, p)

        loop(PIECES, first)

    @pl.when(jnp.logical_not(is_end))
    def _():
        def first(p):
            to_near(t, p)
            to_far(t, p)
            to_across(t, p)

        loop(PIECES, first)

    pair_down.start()
    pair_up.start()

    @pl.when(is_end)
    def _():
        f1, f2, f3 = share(sign, False), share(2 * sign, False), share(3 * sign, False)
        x0, x1 = share(0, True), share(sign, True)
        x2, x3 = share(2 * sign, True), share(3 * sign, True)
        load_w(f1, 1).start()
        load_w(x0, 2).start()

        def phase0(p):
            got(f1, p)
            to_across(f1, p)
            got(x0, p)

            @pl.when(p % 2 == 1)
            def _():
                to_far(x0, p)

            own_tiles(p)

        loop(PIECES, phase0)
        load_w(f2, 0).start()
        rank_partial()

        def phase1(p):
            got(f2, p)
            to_across(f2, p)
            got(x1, p)
            run(4 * p, 4 * p + 4, [(f1, 1), (x0, 2)])

        loop(PIECES, phase1)
        load_w(x1, 1).start()
        load_w(f3, 2).start()
        rank_sum()

        def phase2(p):
            got(f3, p)

            @pl.when(p % 2 == 0)
            def _():
                to_across(f3, p)

            got(x2, p)
            run(4 * p, 4 * p + 4, [(f2, 0), (x1, 1)])

            @pl.when(p == 4)
            def _():
                load_w(x2, 0).start()

            @pl.when(p == 1)
            def _():
                load_w(f3, 2).wait()

            @pl.when(p % 2 == 1)
            def _():
                loop(tiles, lambda k: add(f3, p - 1, 2, 2, k))

        loop(PIECES, phase2)
        load_w(x3, 1).start()
        expand()
        run(0, tiles, [(x2, 0)])
        load_w(x3, 1).wait()

        def phase3(h):
            got(x3, 2 * h)
            got(x3, 2 * h + 1)
            finish(x3, 1, h)

        loop(PIECES // 2, phase3)
        drain(0, 12)
        drain(2, 28)

    @pl.when(jnp.logical_not(is_end))
    def _():
        f1, f2, n1 = share(sign, False), share(2 * sign, False), share(-sign, False)
        x0, x1 = share(0, True), share(sign, True)
        xn, x2 = share(-sign, True), share(2 * sign, True)
        load_w(f1, 1).start()
        load_w(n1, 2).start()

        def phase0(p):
            got(f1, p)
            to_near(f1, p)
            to_across(f1, p)
            got(n1, p)
            to_far(n1, p)

            @pl.when(p % 2 == 0)
            def _():
                to_across(n1, p)

            got(x0, p)
            own_tiles(p)

        loop(PIECES, phase0)
        load_w(x0, 0).start()
        rank_partial()

        def phase1(p):
            got(f2, p)
            to_near(f2, p)

            @pl.when(p % 2 == 0)
            def _():
                to_across(f2, p)

            got(xn, p)

            @pl.when(p % 2 == 1)
            def _():
                to_far(xn, p)

            got(x1, p)
            run(6 * p, 6 * p + 6, [(f1, 1), (n1, 2), (x0, 0)])

            @pl.when(p == 3)
            def _():
                load_w(f2, 1).start()

            @pl.when(p == 5)
            def _():
                load_w(x1, 2).start()

        loop(PIECES, phase1)
        load_w(xn, 0).start()
        rank_sum()

        def phase2(h):
            got(x2, 2 * h)
            got(x2, 2 * h + 1)
            to_near(x2, 2 * h + 1)
            run(12 * h, 12 * h + 12, [(f2, 1), (x1, 2), (xn, 0)])

            @pl.when(h == 2)
            def _():
                load_w(x2, 1).start()

        loop(PIECES // 2, phase2)
        expand()
        load_w(x2, 1).wait()
        loop(PIECES // 2, lambda h: finish(x2, 1, h))
        drain(0, 20)
        drain(1, 28)
        drain(2, 24)

    pair_down.wait_send()
    pair_up.wait_send()

    def sent(d, carry):
        rs_copy(d).wait_send()
        ag_copy(d).wait_send()
        return carry

    lax.fori_loop(1, n, sent, 0)
    loop(PIECES // 2, lambda h: out_copy(h).wait())


def factors(adapter_shrink_weight, adapter_expand_weight, block_adapter_index):
    stores = lax.axis_size("store")
    me = lax.axis_index("store")
    held = adapter_shrink_weight.shape[0]
    step_count = block_adapter_index.shape[0]
    wanted = block_adapter_index.reshape(step_count, stores, -1).transpose(1, 0, 2)
    wanted = wanted.reshape(stores, -1)

    def pick(weight, index):
        kept = (index // held == me)[:, None, None]
        return jnp.where(kept, jnp.take(weight, index % held, axis=0), jnp.zeros((), BF16))

    mine = lax.dynamic_index_in_dim(wanted, me, 0, keepdims=False)
    other = lax.dynamic_index_in_dim(wanted, 1 - me, 0, keepdims=False)
    return tuple(
        pick(weight, index)
        for weight in (adapter_shrink_weight, adapter_expand_weight)
        for index in (mine, other)
    )


def fused(inputs, base_up_matrix, adapter_shrink_weight, adapter_expand_weight, block_adapter_index):
    step_count, rows_dev, depth = inputs.shape
    n = lax.axis_size("tensor")
    rows, hidden = step_count * rows_dev, base_up_matrix.shape[1]
    rank = adapter_shrink_weight.shape[1]
    block = rows // PIECES
    parts = factors(adapter_shrink_weight, adapter_expand_weight, block_adapter_index)
    out = pl.pallas_call(
        kernel,
        out_shape=jax.ShapeDtypeStruct((rows, hidden), BF16),
        in_specs=[pl.BlockSpec(memory_space=pl.ANY)] * 6,
        out_specs=pl.BlockSpec(memory_space=pl.ANY),
        scratch_shapes=[
            pltpu.VMEM((n * PIECES, block, depth), BF16),
            pltpu.VMEM((rows, hidden), F32),
            pltpu.VMEM((3, depth, hidden), BF16),
            pltpu.VMEM((PIECES, 2 * rank, depth), BF16),
            pltpu.VMEM((PIECES, 2 * rank, hidden), BF16),
            pltpu.VMEM((PIECES, rank, block), F32),
            pltpu.VMEM((PIECES, rank, block), F32),
            pltpu.VMEM((PIECES, rank, block), BF16),
            pltpu.SemaphoreType.DMA((3,)),
            pltpu.SemaphoreType.DMA((n * PIECES,)),
            pltpu.SemaphoreType.DMA((3,)),
            pltpu.SemaphoreType.DMA((3,)),
            pltpu.SemaphoreType.DMA((2,)),
            pltpu.SemaphoreType.DMA((2,)),
            pltpu.SemaphoreType.DMA((n,)),
            pltpu.SemaphoreType.DMA((n,)),
            pltpu.SemaphoreType.DMA((n,)),
            pltpu.SemaphoreType.DMA((n,)),
            pltpu.SemaphoreType.DMA((4,)),
        ],
        compiler_params=pltpu.CompilerParams(
            collective_id=0, has_side_effects=True, vmem_limit_bytes=63 * 1024 * 1024
        ),
        cost_estimate=pl.CostEstimate(
            flops=2 * rows * hidden * depth * n, bytes_accessed=100_000_000, transcendentals=0
        ),
    )(inputs.reshape(PIECES, block, depth), base_up_matrix, *parts)
    return out.reshape(step_count, rows_dev, hidden)


def general(
    inputs, base_up_matrix, adapter_shrink_weight, adapter_expand_weight, block_adapter_index
):
    step_count, rows_dev, width_dev = inputs.shape
    hidden_dev = base_up_matrix.shape[1]
    blocks_dev = block_adapter_index.shape[1] // lax.axis_size("store")
    block_rows = rows_dev // blocks_dev
    parts = factors(adapter_shrink_weight, adapter_expand_weight, block_adapter_index)
    swap = [(0, 1), (1, 0)]
    down = parts[0] + lax.ppermute(parts[1], "store", swap)
    up = parts[2] + lax.ppermute(parts[3], "store", swap)
    full_rows = lax.all_gather(
        inputs.reshape(step_count * rows_dev, width_dev), "tensor", axis=1, tiled=True
    )
    own_blocks = inputs.reshape(step_count * blocks_dev, block_rows, width_dev)
    low_rank = jnp.einsum("btd,brd->brt", own_blocks, down, preferred_element_type=F32)
    low_rank = lax.psum(low_rank, "tensor").astype(BF16)
    base_out = jnp.dot(full_rows, base_up_matrix, preferred_element_type=F32)
    adapter_out = jnp.einsum("brt,brf->btf", low_rank, up, preferred_element_type=F32)
    projected = (base_out + adapter_out.reshape(base_out.shape)).astype(BF16)
    return projected.reshape(step_count, rows_dev, hidden_dev)


def solution(mesh):
    placed = (
        P("groups", "store", "tensor"),
        P(None, "tensor"),
        P("store", None, "tensor"),
        P("store", None, "tensor"),
        P("groups", None),
    )
    small = mesh.shape["tensor"] == PIECES and mesh.shape["store"] == 2
    return jax.shard_map(
        fused if small else general,
        mesh=mesh, in_specs=placed, out_specs=P("groups", "store", "tensor"), check_vma=False,
    )
```
